512 devices in a mesh: row: 32 (over y, z_hi), col: 16 (over z_lo, x, core).
Axes of the slice: x: 4, y: 8, z: 8 (z_hi: 4, z_lo: 2; z = z_hi * 2 + z_lo), core: 2. Of those that a mesh axis runs over, the one named last changes fastest.
Arguments:
- three_index: bfloat16 [32, 16, 8, 2, 128, 128], P('row', 'col'), may hold values from -6 to 6
- slot_pair: int32 [32, 16, 8], P('row', 'col'), may hold values from -1 to 31, as said below
- coeff: bfloat16 [16384, 256], P(('col', 'row')), may hold values from -0.125 to 0.125
- occ_mask: int32 [128, 2], P('col'), may hold values 0 or 1
Outputs:
- exchange_block: bfloat16 [16384, 16384], P('row', 'col')
The draws below stay inside these ranges and needn't reach their ends.
Inputs may be any that keep to these rules, and one draw needn't show every extreme that they name: `slot_pair`: on each device (first two dimensions) the 8 slots name distinct local pair blocks mb * 8 + nb, the live ones first and -1 after them; in every draw some device fills all 8 slots.
All inputs are finite; a program needn't handle non-finite values. No bound on the sum of `occ_mask` on one device may be relied on, other than what follows from the above.
Results may differ from the reference program's by a relative error of at most 0.0057.
Values may be sent and summed in bfloat16 or wider, within the bound.
A program may use at most 64 MiB of HBM per device.

```python
import jax
import jax.numpy as jnp
from jax import lax

BLK = 128
MB_DEV = 4
AUX = 2
OCC = 256
KB = 8
NAO = 16384
NB = 128
NBC = 8
NOB = 2
N_ROW = 32
N_COL = 16


def draw_slot_pair(key, part):
    npairs = MB_DEV * NBC
    total = N_ROW * N_COL
    first, second, third, fourth = jax.random.split(key, 4)
    base = jax.random.randint(first, (total,), 1, 4)
    heavy = jax.random.randint(second, (total,), 0, 8) == 0
    counts = jnp.where(heavy, KB, jnp.minimum(base, KB))
    chosen = jax.random.randint(third, (), 0, total)
    counts = counts.at[chosen].set(KB)
    orders = jax.vmap(lambda sub: jax.random.permutation(sub, npairs))(jax.random.split(fourth, total))[:, :KB]
    positions = jnp.arange(KB)[None, :]
    result = jnp.where(positions < counts[:, None], orders, -1)
    return result.reshape(N_ROW, N_COL, KB).astype(jnp.int32)


def with_ends(drawn, rng, least, top_value):
    extent = drawn.shape
    index_at = [jax.random.randint(jax.random.fold_in(rng, axis), (), 0, extent[axis]) for axis in range(len(extent))]
    drawn = drawn.at[tuple(index_at)].set(least)
    longest = extent.index(max(extent))
    index_at[longest] = (index_at[longest] + 1) % extent[longest]
    return drawn.at[tuple(index_at)].set(top_value)


def level_of(rng, dims, pieces, least, largest):
    gain = 1.0
    for dim, parts in pieces:
        draws = jax.random.uniform(jax.random.fold_in(jax.random.fold_in(rng, 6), dim), (parts,), jnp.float32, least / len(pieces), largest / len(pieces))
        gain = gain * jnp.repeat(jnp.exp(draws), dims[dim] // parts).reshape((-1,) + (1,) * (len(dims) - 1 - dim))
    return gain


def bell_draw(key, shape, scale, bound, cuts=(), kind=jnp.bfloat16):
    entries = jax.random.normal(key, shape, jnp.float32) * scale
    if len(cuts) > 0:
        entries = level_of(key, shape, cuts, -0.22, 0.18) * entries
    return jnp.clip(entries, min=-bound, max=bound).astype(kind)


def setup_inputs(seed: int = 0) -> dict:
    keys = jax.random.split(jax.random.key(seed), 5)
    three_index = bell_draw(keys[0], (N_ROW, N_COL, KB, AUX, BLK, BLK), 1.0, 6.0, ((0, 32), (1, 16)))
    slot_pair = draw_slot_pair(jax.random.fold_in(keys[4], 71), 0)
    coeff = bell_draw(keys[2], (NAO, OCC), (BLK * 16) ** -0.5, 0.125, ((0, 512),))
    occ_mask = with_ends((jax.random.randint(keys[3], (NB, NOB), 0, 3) < 2).astype(jnp.int32), jax.random.fold_in(keys[3], 1), 0, 1)
    return {"three_index": three_index, "slot_pair": slot_pair, "coeff": coeff, "occ_mask": occ_mask}


def reference(three_index, slot_pair, coeff, occ_mask):
    keep = occ_mask.astype(coeff.dtype)[:, None, :, None]
    masked = (coeff.reshape(NB, BLK, NOB, BLK) * keep).reshape(NAO, OCC)
    blocks = three_index.reshape(N_ROW * N_COL * KB, AUX, BLK, BLK)
    slots = slot_pair.reshape(N_ROW * N_COL * KB)

    def add_slot(index, half):
        device = index // KB
        row_index = device // N_COL
        col_index = device % N_COL
        pair = slots[index]
        live = (pair >= 0).astype(half.dtype)
        pair = jnp.maximum(pair, 0)
        mu_start = ((row_index * MB_DEV + pair // NBC) * BLK).astype(jnp.int32)
        nu_start = ((col_index * NBC + pair % NBC) * BLK).astype(jnp.int32)
        rows = lax.dynamic_slice_in_dim(masked, nu_start, BLK, 0).astype(half.dtype)
        block = blocks[index].astype(half.dtype)
        term = jnp.einsum('pab,bi->api', block, rows)
        current = lax.dynamic_slice_in_dim(half, mu_start, BLK, 0)
        return lax.dynamic_update_slice_in_dim(half, current + live * term, mu_start, 0)
    half = jnp.zeros((NAO, AUX, OCC), jnp.float32)
    half = lax.fori_loop(0, N_ROW * N_COL * KB, add_slot, half)
    flat = half.astype(jnp.bfloat16).reshape(NAO, AUX * OCC)
    product = jnp.dot(flat, flat.T, preferred_element_type=jnp.float32)
    return (product / jnp.sqrt(jnp.float32(AUX * OCC))).astype(jnp.bfloat16)
```

```python
import jax
import jax.numpy as jnp
from jax import lax
from jax.experimental import pallas as pl
from jax.experimental.pallas import tpu as pltpu
from jax.sharding import PartitionSpec as P

MESH = pl.DeviceIdType.MESH
BF16 = jnp.bfloat16
F32 = jnp.float32
NY, NZH, NX = 8, 4, 4
Y_ORDER = (4, 3, 5, 2, 6, 1, 7)
Z_ORDER = (2, 1, 3)
SCALE = 512.0**-0.5


def kernel(
    slot_ref, mask_ref, coeff_ref, blocks_ref, out_ref,
    blocks, ga, gb, rhs, part, own, theirs, summed, landed, piece, mu, ya, zb, nua, nub, sends, recvs, local,
):
    row, col = lax.axis_index("row"), lax.axis_index("col")
    y, zh = row // NZH, row % NZH
    chip, k = col // 2, col % 2
    zl, x = chip // NX, chip % NX

    def along_y(d):
        return (((y + d) % NY) * NZH + zh, col)

    def along_z(d):
        return (y * NZH + (zh + d) % NZH, col)

    def in_row(d):
        return (row, ((chip + d) % 8) * 2 + k)

    sibling = (row, chip * 2 + 1 - k)

    def send(src, dst, index, device):
        pltpu.make_async_remote_copy(
            src_ref=src, dst_ref=dst, send_sem=sends.at[index], recv_sem=recvs.at[index],
            device_id=device, device_id_type=MESH,
        ).start()

    def took(sems, index, ref):
        pltpu.make_async_copy(ref, ref, sems.at[index]).wait()

    fetch = pltpu.make_async_copy(blocks_ref, blocks, local)
    fetch.start()
    ga[y, zh] = coeff_ref[:, 0:128]
    gb[zh, y] = coeff_ref[:, 128:256]

    barrier = pltpu.get_barrier_semaphore()
    peers = [along_y(d) for d in Y_ORDER] + [along_z(d) for d in Z_ORDER] + [in_row(d) for d in range(1, 8)] + [sibling]
    for peer in peers:
        pl.semaphore_signal(barrier, inc=1, device_id=peer, device_id_type=MESH)
    pl.semaphore_wait(barrier, len(peers))

    for d in Z_ORDER:
        send(ga.at[y, zh], ga.at[y, zh], 0, along_z(d))
    for d in Y_ORDER:
        send(gb.at[zh, y], gb.at[zh, y], 1, along_y(d))
    took(recvs, 0, ga.at[0, pl.ds(0, 3)])
    for d in Y_ORDER:
        send(ga.at[y], ga.at[y], 2, along_y(d))
    took(recvs, 1, gb.at[0, pl.ds(0, 7)])
    for d in Z_ORDER:
        send(gb.at[zh], gb.at[zh], 3, along_z(d))
    fetch.wait()
    took(recvs, 2, ga.at[pl.ds(0, 7)])
    took(recvs, 3, gb.at[pl.ds(0, 3)])

    zeros = jnp.zeros((128, 128), BF16)
    for s in range(8):
        nb = slot_ref[0, 0, s] & 7
        rows = pl.ds(s * 128, 128)
        rhs[rows, 0:128] = jnp.where(mask_ref[nb, 0] != 0, ga[nb].reshape(128, 128), zeros)
        rhs[rows, 128:256] = jnp.where(mask_ref[nb, 1] != 0, gb[:, nb].reshape(128, 128), zeros)

    def partial(mb):
        zero = jnp.zeros((256, 128), BF16)
        lhs = [
            jnp.where((slot_ref[0, 0, s] >> 3) == mb, blocks[s].reshape(256, 128), zero)
            for s in range(8)
        ]
        return jnp.dot(jnp.concatenate(lhs, axis=1), rhs[...], preferred_element_type=F32)

    for j in range(2):
        value = partial((1 - k) * 2 + j).astype(BF16)
        for p in range(2):
            part[pl.ds(j * 128, 128), p * 256 : (p + 1) * 256] = value[p * 128 : (p + 1) * 128]
    send(part, theirs, 4, sibling)
    for j in range(2):
        value = partial(k * 2 + j)
        for p in range(2):
            own[pl.ds(j * 128, 128), p * 256 : (p + 1) * 256] = value[p * 128 : (p + 1) * 128]
    took(recvs, 4, theirs)
    total = own[...] + theirs[...].astype(F32)
    own[...] = total
    summed[...] = total.astype(BF16).reshape(8, 32, 512)
    for d in (6, 2, 5, 7, 1, 3, 4):
        send(summed.at[(chip + d) % 8], landed.at[chip], 5, in_row(d))
    landed[chip] = jnp.zeros((32, 512), BF16)
    took(recvs, 5, landed.at[pl.ds(0, 7)])
    total = own[pl.ds(chip * 32, 32), :]
    for m in range(8):
        total = total + landed[m].astype(F32)
    total = total.astype(BF16)
    place = k * 8 + chip
    for p in range(2):
        piece[p] = total[:, p * 256 : (p + 1) * 256]
    ya[y] = piece[0]
    zb[zh] = piece[1]
    for p in range(2):
        mu[p, place] = piece[p]

    for d in Y_ORDER:
        send(ya.at[y], ya.at[y], 6, along_y(d))
    for d in Z_ORDER:
        send(zb.at[zh], zb.at[zh], 7, along_z(d))
    for d in (6, 2, 5, 7, 1, 3, 4):
        send(piece, mu.at[:, place], 8, in_row(d))
    took(recvs, 7, zb.at[pl.ds(0, 3)])
    at_home = chip == y
    for j in range(NY):
        yy = (y + 4 + j) % NY
        for kk in range(2):
            kt = (k + 1 + kk) % 2
            src, dst = zb.at[pl.ds(kt * 2, 2)], nub.at[:, place]
            target = (yy * NZH + zh, y * 2 + kt)
            if j == 4 and kk == 1:

                @pl.when(at_home)
                def _():
                    pltpu.make_async_copy(src, dst, recvs.at[9]).start()

                @pl.when(jnp.logical_not(at_home))
                def _():
                    send(src, dst, 9, target)
            else:
                send(src, dst, 9, target)
    took(recvs, 6, ya.at[pl.ds(0, 7)])
    same_core = k == zh // 2
    for j in range(NY):
        yp = (chip + 1 + j) % NY
        for d in (2, 1, 3, 0):
            src, dst = ya.at[yp], nua.at[zh % 2, place]
            target = (y * NZH + (zh + d) % NZH, yp * 2 + zh // 2)
            if j == 7 and d == 0:

                @pl.when(same_core)
                def _():
                    pltpu.make_async_copy(src, dst, recvs.at[10]).start()

                @pl.when(jnp.logical_not(same_core))
                def _():
                    send(src, dst, 10, target)
            else:
                send(src, dst, 10, target)
    took(recvs, 8, mu.at[:, pl.ds(0, 7)])
    half = mu.at[:, pl.ds(k * 8, 8)]
    send(half, half, 11, sibling)
    took(recvs, 11, mu.at[:, pl.ds(0, 8)])
    took(recvs, 9, nub)
    took(recvs, 10, nua)

    def dot(left, right):
        return lax.dot_general(left, right, (((1,), (1,)), ((), ())), preferred_element_type=F32)

    for h in range(2):
        for q in range(2):
            right = pl.ds(q * 8, 8)
            value = dot(mu[0].reshape(512, 256), nua[h, right].reshape(256, 256))
            value = value + dot(mu[1].reshape(512, 256), nub[h, right].reshape(256, 256))
            out_ref[:, h * 512 + q * 256 : h * 512 + (q + 1) * 256] = (value * SCALE).astype(BF16)

    took(sends, 0, ga.at[0, pl.ds(0, 3)])
    took(sends, 1, gb.at[0, pl.ds(0, 7)])
    took(sends, 2, ga.at[pl.ds(0, 7)])
    took(sends, 3, gb.at[pl.ds(0, 3)])
    took(sends, 4, theirs)
    took(sends, 5, landed.at[pl.ds(0, 7)])
    took(sends, 6, ya.at[pl.ds(0, 7)])
    took(sends, 7, zb.at[pl.ds(0, 3)])
    took(sends, 8, mu.at[:, pl.ds(0, 7)])
    took(sends, 11, mu.at[:, pl.ds(0, 8)])

    @pl.when(at_home)
    def _():
        took(sends, 9, nub.at[:, pl.ds(0, 15)])

    @pl.when(jnp.logical_not(at_home))
    def _():
        took(sends, 9, nub)

    @pl.when(same_core)
    def _():
        took(sends, 10, nua.at[0, pl.ds(0, 15)])
        took(sends, 10, nua.at[0])

    @pl.when(jnp.logical_not(same_core))
    def _():
        took(sends, 10, nua)


def body(three_index, slot_pair, coeff, occ_mask):
    return pl.pallas_call(
        kernel,
        out_shape=jax.ShapeDtypeStruct((512, 1024), BF16),
        in_specs=[
            pl.BlockSpec(memory_space=pltpu.SMEM),
            pl.BlockSpec(memory_space=pltpu.SMEM),
            pl.BlockSpec(memory_space=pltpu.VMEM),
            pl.BlockSpec(memory_space=pl.ANY),
        ],
        out_specs=pl.BlockSpec(memory_space=pltpu.VMEM),
        scratch_shapes=[
            pltpu.VMEM((8, 2, 128, 128), BF16),
            pltpu.VMEM((8, 4, 32, 128), BF16),
            pltpu.VMEM((4, 8, 32, 128), BF16),
            pltpu.VMEM((1024, 256), BF16),
            pltpu.VMEM((256, 512), BF16),
            pltpu.VMEM((256, 512), F32),
            pltpu.VMEM((256, 512), BF16),
            pltpu.VMEM((8, 32, 512), BF16),
            pltpu.VMEM((8, 32, 512), BF16),
            pltpu.VMEM((2, 32, 256), BF16),
            pltpu.VMEM((2, 16, 32, 256), BF16),
            pltpu.VMEM((8, 32, 256), BF16),
            pltpu.VMEM((4, 32, 256), BF16),
            pltpu.VMEM((2, 16, 32, 256), BF16),
            pltpu.VMEM((2, 16, 32, 256), BF16),
            pltpu.SemaphoreType.DMA((12,)),
            pltpu.SemaphoreType.DMA((12,)),
            pltpu.SemaphoreType.DMA,
        ],
        compiler_params=pltpu.CompilerParams(
            collective_id=0, has_side_effects=True, vmem_limit_bytes=40 * 2**20
        ),
        cost_estimate=pl.CostEstimate(flops=805306368, bytes_accessed=1638400, transcendentals=0),
    )(slot_pair, occ_mask, coeff, three_index.reshape(8, 2, 128, 128))


def solution(mesh):
    return jax.shard_map(
        body,
        mesh=mesh,
        in_specs=(
            P("row", "col", None, None, None, None),
            P("row", "col", None),
            P(("col", "row"), None),
            P("col", None),
        ),
        out_specs=P("row", "col"),
        check_vma=False,
    )
```

```python
import jax
import jax.numpy as jnp
from jax import lax
from jax.experimental import pallas as pl
from jax.experimental.pallas import tpu as pltpu
from jax.sharding import PartitionSpec as P

MESH = pl.DeviceIdType.MESH
BF16 = jnp.bfloat16
F32 = jnp.float32
NY, NZH, NX = 8, 4, 4
Y_ORDER = (4, 3, 5, 2, 6, 1, 7)
Z_ORDER = (2, 1, 3)
SCALE = 512.0**-0.5


def kernel(
    slot_hbm, mask_hbm, coeff_hbm, blocks_hbm, out_ref,
    slot_ref, mask_ref, coeff_ref, blocks,
    ga, gb, rhs, part, own, theirs, summed, landed, piece, mu, ya, zb, nua, nub, sends, recvs, local,
):
    row, col = lax.axis_index("row"), lax.axis_index("col")
    y, zh = row // NZH, row % NZH
    chip, k = col // 2, col % 2
    zl, x = chip // NX, chip % NX

    def along_y(d):
        return (((y + d) % NY) * NZH + zh, col)

    def along_z(d):
        return (y * NZH + (zh + d) % NZH, col)

    def in_row(d):
        return (row, ((chip + d) % 8) * 2 + k)

    sibling = (row, chip * 2 + 1 - k)

    def send(src, dst, index, device):
        pltpu.make_async_remote_copy(
            src_ref=src, dst_ref=dst, send_sem=sends.at[index], recv_sem=recvs.at[index],
            device_id=device, device_id_type=MESH,
        ).start()

    def took(sems, index, ref):
        pltpu.make_async_copy(ref, ref, sems.at[index]).wait()

    fetches = [
        pltpu.make_async_copy(src, dst, local.at[n])
        for n, (src, dst) in enumerate(
            ((coeff_hbm, coeff_ref), (slot_hbm, slot_ref), (mask_hbm, mask_ref), (blocks_hbm, blocks))
        )
    ]
    for fetch in fetches:
        fetch.start()
    barrier = pltpu.get_barrier_semaphore()
    peers = [along_y(d) for d in Y_ORDER] + [along_z(d) for d in Z_ORDER] + [in_row(d) for d in range(1, 8)] + [sibling]
    for peer in peers:
        pl.semaphore_signal(barrier, inc=1, device_id=peer, device_id_type=MESH)
    fetches[0].wait()
    ga[y, zh] = coeff_ref[:, 0:128]
    gb[zh, y] = coeff_ref[:, 128:256]
    pl.semaphore_wait(barrier, len(peers))

    for d in Z_ORDER:
        send(ga.at[y, zh], ga.at[y, zh], 0, along_z(d))
    for d in Y_ORDER:
        send(gb.at[zh, y], gb.at[zh, y], 1, along_y(d))
    took(recvs, 0, ga.at[0, pl.ds(0, 3)])
    for d in Y_ORDER:
        send(ga.at[y], ga.at[y], 2, along_y(d))
    took(recvs, 1, gb.at[0, pl.ds(0, 7)])
    for d in Z_ORDER:
        send(gb.at[zh], gb.at[zh], 3, along_z(d))
    for fetch in fetches[1:]:
        fetch.wait()
    took(recvs, 2, ga.at[pl.ds(0, 7)])
    took(recvs, 3, gb.at[pl.ds(0, 3)])

    zeros = jnp.zeros((128, 128), BF16)
    for s in range(8):
        nb = slot_ref[0, 0, s] & 7
        rows = pl.ds(s * 128, 128)
        rhs[rows, 0:128] = jnp.where(mask_ref[0, nb] != 0, ga[nb].reshape(128, 128), zeros)
        rhs[rows, 128:256] = jnp.where(mask_ref[1, nb] != 0, gb[:, nb].reshape(128, 128), zeros)

    def partial(mb):
        zero = jnp.zeros((256, 128), BF16)
        lhs = [
            jnp.where((slot_ref[0, 0, s] >> 3) == mb, blocks[s].reshape(256, 128), zero)
            for s in range(8)
        ]
        return jnp.dot(jnp.concatenate(lhs, axis=1), rhs[...], preferred_element_type=F32)

    for j in range(2):
        value = partial((1 - k) * 2 + j).astype(BF16)
        for p in range(2):
            part[pl.ds(j * 128, 128), p * 256 : (p + 1) * 256] = value[p * 128 : (p + 1) * 128]
    send(part, theirs, 4, sibling)
    for j in range(2):
        value = partial(k * 2 + j)
        for p in range(2):
            own[pl.ds(j * 128, 128), p * 256 : (p + 1) * 256] = value[p * 128 : (p + 1) * 128]
    took(recvs, 4, theirs)
    total = own[...] + theirs[...].astype(F32)
    own[...] = total
    summed[...] = total.astype(BF16).reshape(8, 32, 512)
    for d in (6, 2, 5, 7, 1, 3, 4):
        send(summed.at[(chip + d) % 8], landed.at[chip], 5, in_row(d))
    landed[chip] = jnp.zeros((32, 512), BF16)
    took(recvs, 5, landed.at[pl.ds(0, 7)])
    total = own[pl.ds(chip * 32, 32), :]
    for m in range(8):
        total = total + landed[m].astype(F32)
    total = total.astype(BF16)
    place = k * 8 + chip
    for q in range(4):
        block = total[:, q * 128 : (q + 1) * 128]
        piece[q] = block
        mu[q, place] = block
        if q == 0:
            ya[y] = block
        else:
            zb[zh, q - 1] = block

    for d in Y_ORDER:
        send(ya.at[y], ya.at[y], 6, along_y(d))
    for d in Z_ORDER:
        send(zb.at[zh], zb.at[zh], 7, along_z(d))
    for d in (6, 2, 5, 7, 1, 3, 4):
        send(piece, mu.at[:, place], 8, in_row(d))
    took(recvs, 7, zb.at[pl.ds(0, 3)])
    at_home = chip == y
    for j in range(NY):
        yy = (y + 4 + j) % NY
        for kk in range(2):
            kt = (k + 1 + kk) % 2
            src, dst = zb.at[pl.ds(kt * 2, 2)], nub.at[:, :, place]
            target = (yy * NZH + zh, y * 2 + kt)
            if j == 4 and kk == 1:

                @pl.when(at_home)
                def _():
                    pltpu.make_async_copy(src, dst, recvs.at[9]).start()

                @pl.when(jnp.logical_not(at_home))
                def _():
                    send(src, dst, 9, target)
            else:
                send(src, dst, 9, target)
    took(recvs, 6, ya.at[pl.ds(0, 7)])
    same_core = k == zh // 2
    for j in range(NY):
        yp = (chip + 1 + j) % NY
        for d in (2, 1, 3, 0):
            src, dst = ya.at[yp], nua.at[zh % 2, place]
            target = (y * NZH + (zh + d) % NZH, yp * 2 + zh // 2)
            if j == 7 and d == 0:

                @pl.when(same_core)
                def _():
                    pltpu.make_async_copy(src, dst, recvs.at[10]).start()

                @pl.when(jnp.logical_not(same_core))
                def _():
                    send(src, dst, 10, target)
            else:
                send(src, dst, 10, target)
    took(recvs, 8, mu.at[:, pl.ds(0, 7)])
    half = mu.at[:, pl.ds(k * 8, 8)]
    send(half, half, 11, sibling)
    took(recvs, 11, mu.at[:, pl.ds(0, 8)])
    took(recvs, 9, nub)
    took(recvs, 10, nua)

    def dot(left, right):
        return lax.dot_general(left, right, (((1,), (1,)), ((), ())), preferred_element_type=F32)

    left = jnp.concatenate([mu[q].reshape(512, 128) for q in range(4)], axis=1)
    for h in range(2):
        for n in range(2):
            at = pl.ds(n * 8, 8)
            right = [nua[h, at]] + [nub[h, q, at] for q in range(3)]
            value = dot(left, jnp.concatenate([v.reshape(256, 128) for v in right], axis=1))
            out_ref[:, h * 512 + n * 256 : h * 512 + (n + 1) * 256] = (value * SCALE).astype(BF16)

    took(sends, 0, ga.at[0, pl.ds(0, 3)])
    took(sends, 1, gb.at[0, pl.ds(0, 7)])
    took(sends, 2, ga.at[pl.ds(0, 7)])
    took(sends, 3, gb.at[pl.ds(0, 3)])
    took(sends, 4, theirs)
    took(sends, 5, landed.at[pl.ds(0, 7)])
    took(sends, 6, ya.at[pl.ds(0, 7)])
    took(sends, 7, zb.at[pl.ds(0, 3)])
    took(sends, 8, mu.at[:, pl.ds(0, 7)])
    took(sends, 11, mu.at[:, pl.ds(0, 8)])

    @pl.when(at_home)
    def _():
        took(sends, 9, nub.at[:, :, pl.ds(0, 15)])

    @pl.when(jnp.logical_not(at_home))
    def _():
        took(sends, 9, nub)

    @pl.when(same_core)
    def _():
        took(sends, 10, nua.at[0, pl.ds(0, 15)])
        took(sends, 10, nua.at[0])

    @pl.when(jnp.logical_not(same_core))
    def _():
        took(sends, 10, nua)


def body(three_index, slot_pair, coeff, occ_mask):
    arrays = (slot_pair, occ_mask.T, coeff, three_index.reshape(8, 2, 128, 128))
    return pl.pallas_call(
        kernel,
        out_shape=jax.ShapeDtypeStruct((512, 1024), BF16),
        in_specs=[
            pl.BlockSpec(memory_space=pltpu.HBM),
            pl.BlockSpec(memory_space=pltpu.HBM),
            pl.BlockSpec(memory_space=pltpu.HBM),
            pl.BlockSpec(memory_space=pltpu.HBM),
        ],
        out_specs=pl.BlockSpec(memory_space=pltpu.VMEM),
        scratch_shapes=[
            pltpu.SMEM((1, 1, 8), jnp.int32),
            pltpu.SMEM((2, 8), jnp.int32),
            pltpu.VMEM((32, 256), BF16),
            pltpu.VMEM((8, 2, 128, 128), BF16),
            pltpu.VMEM((8, 4, 32, 128), BF16),
            pltpu.VMEM((4, 8, 32, 128), BF16),
            pltpu.VMEM((1024, 256), BF16),
            pltpu.VMEM((256, 512), BF16),
            pltpu.VMEM((256, 512), F32),
            pltpu.VMEM((256, 512), BF16),
            pltpu.VMEM((8, 32, 512), BF16),
            pltpu.VMEM((8, 32, 512), BF16),
            pltpu.VMEM((4, 32, 128), BF16),
            pltpu.VMEM((4, 16, 32, 128), BF16),
            pltpu.VMEM((8, 32, 128), BF16),
            pltpu.VMEM((4, 3, 32, 128), BF16),
            pltpu.VMEM((2, 16, 32, 128), BF16),
            pltpu.VMEM((2, 3, 16, 32, 128), BF16),
            pltpu.SemaphoreType.DMA((12,)),
            pltpu.SemaphoreType.DMA((12,)),
            pltpu.SemaphoreType.DMA((4,)),
        ],
        compiler_params=pltpu.CompilerParams(
            collective_id=0, has_side_effects=True, vmem_limit_bytes=40 * 2**20
        ),
        cost_estimate=pl.CostEstimate(flops=805306368, bytes_accessed=1638400, transcendentals=0),
    )(*(pltpu.with_memory_space_constraint(v, pltpu.HBM) for v in arrays))


def solution(mesh):
    return jax.shard_map(
        body,
        mesh=mesh,
        in_specs=(
            P("row", "col", None, None, None, None),
            P("row", "col", None),
            P(("col", "row"), None),
            P("col", None),
        ),
        out_specs=P("row", "col"),
        check_vma=False,
    )
```

```python
import jax
import jax.numpy as jnp
from jax import lax
from jax.experimental import pallas as pl
from jax.experimental.pallas import tpu as pltpu
from jax.sharding import PartitionSpec as P

MESH = pl.DeviceIdType.MESH
BF16 = jnp.bfloat16
F32 = jnp.float32
NY, NZH, NX = 8, 4, 4
Y_ORDER = (4, 3, 5, 2, 6, 1, 7)
Z_ORDER = (2, 1, 3)
A_ORDER_P = (6, 1, 3, 2, 5, 7, 4, 0)
A_ORDER_Z = (2, 1, 3, 0)
SCALE = 512.0**-0.5


def kernel(
    slot_hbm, mask_hbm, coeff_hbm, blocks_hbm, out_ref,
    slot_ref, mask_ref, coeff_ref, blocks,
    ga, gb, rhs, part, own, theirs, summed, landed, piece, mu, ya, zb, nua, nub, sends, recvs, local,
):
    row, col = lax.axis_index("row"), lax.axis_index("col")
    y, zh = row // NZH, row % NZH
    chip, k = col // 2, col % 2
    zl, x = chip // NX, chip % NX

    def along_y(d):
        return (((y + d) % NY) * NZH + zh, col)

    def along_z(d):
        return (y * NZH + (zh + d) % NZH, col)

    def in_row(d):
        return (row, ((chip + d) % 8) * 2 + k)

    sibling = (row, chip * 2 + 1 - k)

    def send(src, dst, index, device):
        pltpu.make_async_remote_copy(
            src_ref=src, dst_ref=dst, send_sem=sends.at[index], recv_sem=recvs.at[index],
            device_id=device, device_id_type=MESH,
        ).start()

    def took(sems, index, ref):
        pltpu.make_async_copy(ref, ref, sems.at[index]).wait()

    fetches = [
        pltpu.make_async_copy(src, dst, local.at[n])
        for n, (src, dst) in enumerate(
            ((coeff_hbm, coeff_ref), (slot_hbm, slot_ref), (mask_hbm, mask_ref), (blocks_hbm, blocks))
        )
    ]
    for fetch in fetches:
        fetch.start()
    barrier = pltpu.get_barrier_semaphore()
    peers = [along_y(d) for d in Y_ORDER] + [along_z(d) for d in Z_ORDER] + [in_row(d) for d in range(1, 8)] + [sibling]
    for peer in peers:
        pl.semaphore_signal(barrier, inc=1, device_id=peer, device_id_type=MESH)
    fetches[0].wait()
    ga[y, zh] = coeff_ref[:, 0:128]
    gb[zh, y] = coeff_ref[:, 128:256]
    pl.semaphore_wait(barrier, len(peers))

    for d in Z_ORDER:
        send(ga.at[y, zh], ga.at[y, zh], 0, along_z(d))
    for d in Y_ORDER:
        send(gb.at[zh, y], gb.at[zh, y], 1, along_y(d))
    took(recvs, 0, ga.at[0, pl.ds(0, 3)])
    for d in Y_ORDER:
        send(ga.at[y], ga.at[y], 2, along_y(d))
    took(recvs, 1, gb.at[0, pl.ds(0, 7)])
    for d in Z_ORDER:
        send(gb.at[zh], gb.at[zh], 3, along_z(d))
    for fetch in fetches[1:]:
        fetch.wait()
    took(recvs, 2, ga.at[pl.ds(0, 7)])
    took(recvs, 3, gb.at[pl.ds(0, 3)])

    zeros = jnp.zeros((128, 128), BF16)
    for s in range(8):
        nb = slot_ref[0, 0, s] & 7
        rows = pl.ds(s * 128, 128)
        rhs[rows, 0:128] = jnp.where(mask_ref[0, nb] != 0, ga[nb].reshape(128, 128), zeros)
        rhs[rows, 128:256] = jnp.where(mask_ref[1, nb] != 0, gb[:, nb].reshape(128, 128), zeros)

    def partial(mb):
        zero = jnp.zeros((256, 128), BF16)
        lhs = [
            jnp.where((slot_ref[0, 0, s] >> 3) == mb, blocks[s].reshape(256, 128), zero)
            for s in range(8)
        ]
        return jnp.dot(jnp.concatenate(lhs, axis=1), rhs[...], preferred_element_type=F32)

    for j in range(2):
        value = partial((1 - k) * 2 + j).astype(BF16)
        for p in range(2):
            part[pl.ds(j * 128, 128), p * 256 : (p + 1) * 256] = value[p * 128 : (p + 1) * 128]
    send(part, theirs, 4, sibling)
    for j in range(2):
        value = partial(k * 2 + j)
        for p in range(2):
            own[pl.ds(j * 128, 128), p * 256 : (p + 1) * 256] = value[p * 128 : (p + 1) * 128]
    took(recvs, 4, theirs)
    total = own[...] + theirs[...].astype(F32)
    own[...] = total
    summed[...] = total.astype(BF16).reshape(8, 32, 512)
    for d in (6, 2, 5, 7, 1, 3, 4):
        send(summed.at[(chip + d) % 8], landed.at[chip], 5, in_row(d))
    landed[chip] = jnp.zeros((32, 512), BF16)
    took(recvs, 5, landed.at[pl.ds(0, 7)])
    total = own[pl.ds(chip * 32, 32), :]
    for m in range(8):
        total = total + landed[m].astype(F32)
    total = total.astype(BF16)
    place = k * 8 + chip
    for q in range(4):
        block = total[:, q * 128 : (q + 1) * 128]
        piece[q] = block
        mu[q, place] = block
        if q < 2:
            ya[y, q] = block

    at_home, same_core = chip == y, k == zh // 2

    def deliver(src, dst, index, device, here):
        if here is None:
            send(src, dst, index, device)
            return

        @pl.when(here)
        def _():
            pltpu.make_async_copy(src, dst, recvs.at[index]).start()

        @pl.when(jnp.logical_not(here))
        def _():
            send(src, dst, index, device)

    late = piece.at[pl.ds(2, 2)]
    for dz in (2, 1, 3, 0):
        target = (chip * NZH + (zh + dz) % NZH, y * 2 + zh // 2)
        deliver(late, zb.at[zh % 2, :, k], 7, target, at_home & same_core if dz == 0 else None)
    for d in Y_ORDER:
        send(ya.at[y], ya.at[y], 6, along_y(d))
    for d in (6, 2, 5, 7, 1, 3, 4):
        send(piece, mu.at[:, place], 8, in_row(d))
    took(recvs, 6, ya.at[pl.ds(0, 7)])
    for dz in A_ORDER_Z:
        for dp in A_ORDER_P:
            yp = (chip + dp) % NY
            target = (y * NZH + (zh + dz) % NZH, yp * 2 + zh // 2)
            here = same_core if (dp, dz) == (0, 0) else None
            deliver(ya.at[yp], nua.at[zh % 2, :, place], 10, target, here)
    took(recvs, 7, zb)
    for d in Y_ORDER:
        send(zb, nub.at[:, :, :, y], 9, along_y(d))
    nub[:, :, :, y] = zb[...]
    took(recvs, 8, mu.at[:, pl.ds(0, 7)])
    half = mu.at[:, pl.ds(k * 8, 8)]
    send(half, half, 11, sibling)
    took(recvs, 11, mu.at[:, pl.ds(0, 8)])
    took(recvs, 9, nub.at[:, :, :, pl.ds(0, 7)])
    took(recvs, 10, nua)

    def dot(left, right):
        return lax.dot_general(left, right, (((1,), (1,)), ((), ())), preferred_element_type=F32)

    left = jnp.concatenate([mu[q].reshape(512, 128) for q in range(4)], axis=1)
    for h in range(2):
        for n in range(2):
            at = pl.ds(n * 8, 8)
            right = [nua[h, q, at] for q in range(2)] + [nub[h, q, n] for q in range(2)]
            value = dot(left, jnp.concatenate([v.reshape(256, 128) for v in right], axis=1))
            out_ref[:, h * 512 + n * 256 : h * 512 + (n + 1) * 256] = (value * SCALE).astype(BF16)

    took(sends, 0, ga.at[0, pl.ds(0, 3)])
    took(sends, 1, gb.at[0, pl.ds(0, 7)])
    took(sends, 2, ga.at[pl.ds(0, 7)])
    took(sends, 3, gb.at[pl.ds(0, 3)])
    took(sends, 4, theirs)
    took(sends, 5, landed.at[pl.ds(0, 7)])
    took(sends, 6, ya.at[pl.ds(0, 7)])
    took(sends, 9, nub.at[:, :, :, pl.ds(0, 7)])
    took(sends, 8, mu.at[:, pl.ds(0, 7)])
    took(sends, 11, mu.at[:, pl.ds(0, 8)])

    @pl.when(at_home & same_core)
    def _():
        took(sends, 7, zb.at[:, :, 0])
        took(sends, 7, zb.at[0, :, 0])

    @pl.when(jnp.logical_not(at_home & same_core))
    def _():
        took(sends, 7, zb)

    @pl.when(same_core)
    def _():
        took(sends, 10, nua.at[0, :, pl.ds(0, 15)])
        took(sends, 10, nua.at[0])

    @pl.when(jnp.logical_not(same_core))
    def _():
        took(sends, 10, nua)


def body(three_index, slot_pair, coeff, occ_mask):
    arrays = (slot_pair, occ_mask.T, coeff, three_index.reshape(8, 2, 128, 128))
    return pl.pallas_call(
        kernel,
        out_shape=jax.ShapeDtypeStruct((512, 1024), BF16),
        in_specs=[
            pl.BlockSpec(memory_space=pltpu.HBM),
            pl.BlockSpec(memory_space=pltpu.HBM),
            pl.BlockSpec(memory_space=pltpu.HBM),
            pl.BlockSpec(memory_space=pltpu.HBM),
        ],
        out_specs=pl.BlockSpec(memory_space=pltpu.VMEM),
        scratch_shapes=[
            pltpu.SMEM((1, 1, 8), jnp.int32),
            pltpu.SMEM((2, 8), jnp.int32),
            pltpu.VMEM((32, 256), BF16),
            pltpu.VMEM((8, 2, 128, 128), BF16),
            pltpu.VMEM((8, 4, 32, 128), BF16),
            pltpu.VMEM((4, 8, 32, 128), BF16),
            pltpu.VMEM((1024, 256), BF16),
            pltpu.VMEM((256, 512), BF16),
            pltpu.VMEM((256, 512), F32),
            pltpu.VMEM((256, 512), BF16),
            pltpu.VMEM((8, 32, 512), BF16),
            pltpu.VMEM((8, 32, 512), BF16),
            pltpu.VMEM((4, 32, 128), BF16),
            pltpu.VMEM((4, 16, 32, 128), BF16),
            pltpu.VMEM((8, 2, 32, 128), BF16),
            pltpu.VMEM((2, 2, 2, 32, 128), BF16),
            pltpu.VMEM((2, 2, 16, 32, 128), BF16),
            pltpu.VMEM((2, 2, 2, 8, 32, 128), BF16),
            pltpu.SemaphoreType.DMA((12,)),
            pltpu.SemaphoreType.DMA((12,)),
            pltpu.SemaphoreType.DMA((4,)),
        ],
        compiler_params=pltpu.CompilerParams(
            collective_id=0, has_side_effects=True, vmem_limit_bytes=40 * 2**20
        ),
        cost_estimate=pl.CostEstimate(flops=805306368, bytes_accessed=1638400, transcendentals=0),
    )(*(pltpu.with_memory_space_constraint(v, pltpu.HBM) for v in arrays))


def solution(mesh):
    return jax.shard_map(
        body,
        mesh=mesh,
        in_specs=(
            P("row", "col", None, None, None, None),
            P("row", "col", None),
            P(("col", "row"), None),
            P("col", None),
        ),
        out_specs=P("row", "col"),
        check_vma=False,
    )
```

```python
import jax
import jax.numpy as jnp
from jax import lax
from jax.experimental import pallas as pl
from jax.experimental.pallas import tpu as pltpu
from jax.sharding import PartitionSpec as P

MESH = pl.DeviceIdType.MESH
BF16 = jnp.bfloat16
F32 = jnp.float32
NY, NZH, NX = 8, 4, 4
Y_ORDER = (4, 3, 5, 2, 6, 1, 7)
Z_ORDER = (2, 1, 3)
A_ORDER_P = (6, 1, 3, 2, 5, 7, 4, 0)
A_ORDER_Z = (2, 1, 3, 0)
SCALE = 512.0**-0.5


def kernel(
    slot_hbm, mask_hbm, coeff_hbm, blocks_hbm, out_ref,
    slot_ref, mask_ref, coeff_ref, blocks,
    ga0, ga1, gb0, gb1, lhs, rhs, part, own, theirs, summed, landed, piece, mu, ya, zb, nua, nub, sends, recvs, local,
):
    row, col = lax.axis_index("row"), lax.axis_index("col")
    ga, gb = (ga0, ga1), (gb0, gb1)
    y, zh = row // NZH, row % NZH
    chip, k = col // 2, col % 2
    zl, x = chip // NX, chip % NX

    def along_y(d):
        return (((y + d) % NY) * NZH + zh, col)

    def along_z(d):
        return (y * NZH + (zh + d) % NZH, col)

    def in_row(d):
        return (row, ((chip + d) % 8) * 2 + k)

    sibling = (row, chip * 2 + 1 - k)

    def send(src, dst, o, index, device):
        pltpu.make_async_remote_copy(
            src_ref=src, dst_ref=dst, send_sem=sends.at[o, index], recv_sem=recvs.at[o, index],
            device_id=device, device_id_type=MESH,
        ).start()

    def took(sems, o, index, ref):
        pltpu.make_async_copy(ref, ref, sems.at[o, index]).wait()

    fetches = [
        pltpu.make_async_copy(src, dst, local.at[n])
        for n, (src, dst) in enumerate(
            ((coeff_hbm, coeff_ref), (slot_hbm, slot_ref), (mask_hbm, mask_ref), (blocks_hbm, blocks))
        )
    ]
    for fetch in fetches:
        fetch.start()
    barrier = pltpu.get_barrier_semaphore()
    peers = [along_y(d) for d in Y_ORDER] + [along_z(d) for d in Z_ORDER] + [in_row(d) for d in range(1, 8)] + [sibling]
    for peer in peers:
        pl.semaphore_signal(barrier, inc=1, device_id=peer, device_id_type=MESH)
    fetches[0].wait()
    for o in range(2):
        ga[o][y, zh] = coeff_ref[0:16, o * 128 : (o + 1) * 128]
        gb[o][zh, y] = coeff_ref[16:32, o * 128 : (o + 1) * 128]
    pl.semaphore_wait(barrier, len(peers))

    for o in range(2):
        for d in Z_ORDER:
            send(ga[o].at[y, zh], ga[o].at[y, zh], o, 0, along_z(d))
        for d in Y_ORDER:
            send(gb[o].at[zh, y], gb[o].at[zh, y], o, 1, along_y(d))
    for fetch in fetches[1:]:
        fetch.wait()
    zero = jnp.zeros((256, 128), BF16)
    for mb in range(4):
        for s in range(8):
            here = (slot_ref[0, 0, s] >> 3) == mb
            lhs[mb, :, s * 128 : (s + 1) * 128] = jnp.where(here, blocks[s].reshape(256, 128), zero)
    for o in range(2):
        took(recvs, o, 0, ga[o].at[0, pl.ds(0, 3)])
        for d in Y_ORDER:
            send(ga[o].at[y], ga[o].at[y], o, 2, along_y(d))
        took(recvs, o, 1, gb[o].at[0, pl.ds(0, 7)])
        for d in Z_ORDER:
            send(gb[o].at[zh], gb[o].at[zh], o, 3, along_z(d))

    def partial(o, first):
        left = lhs[pl.ds(first, 2)].reshape(512, 1024)
        return jnp.dot(left, rhs[o], preferred_element_type=F32).reshape(2, 2, 128, 128)

    def expand(o):
        took(recvs, o, 2, ga[o].at[pl.ds(0, 7)])
        took(recvs, o, 3, gb[o].at[pl.ds(0, 3)])
        for s in range(8):
            nb = slot_ref[0, 0, s] & 7
            rows = jnp.concatenate([ga[o][nb], gb[o][:, nb]], axis=1).reshape(128, 128)
            rhs[o, s * 128 : (s + 1) * 128, :] = jnp.where(mask_ref[o, nb] != 0, rows, jnp.zeros((128, 128), BF16))
        value = partial(o, (1 - k) * 2).astype(BF16)
        for j in range(2):
            for p in range(2):
                part[o, j * 128 : (j + 1) * 128, p * 128 : (p + 1) * 128] = value[j, p]
        send(part.at[o], theirs.at[o], o, 4, sibling)
        value = partial(o, k * 2)
        for j in range(2):
            for p in range(2):
                own[o, j * 128 : (j + 1) * 128, p * 128 : (p + 1) * 128] = value[j, p]
        landed[o, chip] = jnp.zeros((32, 256), BF16)
        took(recvs, o, 4, theirs.at[o])
        total = own[o] + theirs[o].astype(F32)
        own[o] = total
        summed[o] = total.astype(BF16).reshape(8, 32, 256)
        for d in (6, 2, 5, 7, 1, 3, 4):
            send(summed.at[o, (chip + d) % 8], landed.at[o, chip], o, 5, in_row(d))

    place = k * 8 + chip
    at_home, same_core = chip == y, k == zh // 2

    def deliver(src, dst, o, index, device, here):
        if here is None:
            send(src, dst, o, index, device)
            return

        @pl.when(here)
        def _():
            pltpu.make_async_copy(src, dst, recvs.at[o, index]).start()

        @pl.when(jnp.logical_not(here))
        def _():
            send(src, dst, o, index, device)

    def spread(o):
        took(recvs, o, 5, landed.at[o, pl.ds(0, 7)])
        total = own[o, pl.ds(chip * 32, 32), :]
        for m in range(8):
            total = total + landed[o, m].astype(F32)
        total = total.astype(BF16)
        for p in range(2):
            block = total[:, p * 128 : (p + 1) * 128]
            piece[o, p] = block
            mu[o, p, place] = block
        ya[o, y] = total[:, 0:128]
        for dz in (2, 1, 3, 0):
            target = (chip * NZH + (zh + dz) % NZH, y * 2 + zh // 2)
            here = at_home & same_core if dz == 0 else None
            deliver(piece.at[o, 1], zb.at[o, zh % 2, k], o, 7, target, here)
        for d in Y_ORDER:
            send(ya.at[o, y], ya.at[o, y], o, 6, along_y(d))
        for d in (6, 2, 5, 7, 1, 3, 4):
            send(piece.at[o], mu.at[o, :, place], o, 8, in_row(d))

    def within_plane(o):
        took(recvs, o, 6, ya.at[o, pl.ds(0, 7)])
        for dz in A_ORDER_Z:
            for dp in A_ORDER_P:
                yp = (chip + dp) % NY
                target = (y * NZH + (zh + dz) % NZH, yp * 2 + zh // 2)
                here = same_core if (dp, dz) == (0, 0) else None
                deliver(ya.at[o, yp], nua.at[o, zh % 2, place], o, 10, target, here)

    def over_y(o):
        took(recvs, o, 7, zb.at[o])
        for d in Y_ORDER:
            send(zb.at[o], nub.at[o, :, :, y], o, 9, along_y(d))
        nub[o, :, :, y] = zb[o]

    expand(0)
    expand(1)
    spread(0)
    spread(1)
    within_plane(0)
    over_y(0)
    within_plane(1)
    over_y(1)
    for o in range(2):
        took(recvs, o, 8, mu.at[o, :, pl.ds(0, 7)])
        half = mu.at[o, :, pl.ds(k * 8, 8)]
        send(half, half, o, 11, sibling)
    for o in range(2):
        took(recvs, o, 11, mu.at[o, :, pl.ds(0, 8)])
        took(recvs, o, 9, nub.at[o, :, :, pl.ds(0, 7)])
        took(recvs, o, 10, nua.at[o])

    def dot(left, right):
        return lax.dot_general(left, right, (((1,), (1,)), ((), ())), preferred_element_type=F32)

    left = jnp.concatenate([mu[o, p].reshape(512, 128) for o in range(2) for p in range(2)], axis=1)
    for h in range(2):
        for n in range(2):
            right = []
            for o in range(2):
                right += [nua[o, h, pl.ds(n * 8, 8)].reshape(256, 128), nub[o, h, n].reshape(256, 128)]
            value = dot(left, jnp.concatenate(right, axis=1))
            out_ref[:, h * 512 + n * 256 : h * 512 + (n + 1) * 256] = (value * SCALE).astype(BF16)

    for o in range(2):
        took(sends, o, 0, ga[o].at[0, pl.ds(0, 3)])
        took(sends, o, 1, gb[o].at[0, pl.ds(0, 7)])
        took(sends, o, 2, ga[o].at[pl.ds(0, 7)])
        took(sends, o, 3, gb[o].at[pl.ds(0, 3)])
        took(sends, o, 4, theirs.at[o])
        took(sends, o, 5, landed.at[o, pl.ds(0, 7)])
        took(sends, o, 6, ya.at[o, pl.ds(0, 7)])
        took(sends, o, 8, mu.at[o, :, pl.ds(0, 7)])
        took(sends, o, 9, nub.at[o, :, :, pl.ds(0, 7)])
        took(sends, o, 11, mu.at[o, :, pl.ds(0, 8)])

    @pl.when(at_home & same_core)
    def _():
        for o in range(2):
            took(sends, o, 7, zb.at[o, 0])
            took(sends, o, 7, zb.at[o, 0, 0])

    @pl.when(jnp.logical_not(at_home & same_core))
    def _():
        for o in range(2):
            took(sends, o, 7, zb.at[o])

    @pl.when(same_core)
    def _():
        for o in range(2):
            took(sends, o, 10, nua.at[o, 0, pl.ds(0, 15)])
            took(sends, o, 10, nua.at[o, 0])

    @pl.when(jnp.logical_not(same_core))
    def _():
        for o in range(2):
            took(sends, o, 10, nua.at[o])


def body(three_index, slot_pair, coeff, occ_mask):
    arrays = (slot_pair, occ_mask.T, coeff, three_index.reshape(8, 2, 128, 128))
    return pl.pallas_call(
        kernel,
        out_shape=jax.ShapeDtypeStruct((512, 1024), BF16),
        in_specs=[
            pl.BlockSpec(memory_space=pltpu.HBM),
            pl.BlockSpec(memory_space=pltpu.HBM),
            pl.BlockSpec(memory_space=pltpu.HBM),
            pl.BlockSpec(memory_space=pltpu.HBM),
        ],
        out_specs=pl.BlockSpec(memory_space=pltpu.VMEM),
        scratch_shapes=[
            pltpu.SMEM((1, 1, 8), jnp.int32),
            pltpu.SMEM((2, 8), jnp.int32),
            pltpu.VMEM((32, 256), BF16),
            pltpu.VMEM((8, 2, 128, 128), BF16),
            pltpu.VMEM((8, 4, 16, 128), BF16),
            pltpu.VMEM((8, 4, 16, 128), BF16),
            pltpu.VMEM((4, 8, 16, 128), BF16),
            pltpu.VMEM((4, 8, 16, 128), BF16),
            pltpu.VMEM((4, 256, 1024), BF16),
            pltpu.VMEM((2, 1024, 128), BF16),
            pltpu.VMEM((2, 256, 256), BF16),
            pltpu.VMEM((2, 256, 256), F32),
            pltpu.VMEM((2, 256, 256), BF16),
            pltpu.VMEM((2, 8, 32, 256), BF16),
            pltpu.VMEM((2, 8, 32, 256), BF16),
            pltpu.VMEM((2, 2, 32, 128), BF16),
            pltpu.VMEM((2, 2, 16, 32, 128), BF16),
            pltpu.VMEM((2, 8, 32, 128), BF16),
            pltpu.VMEM((2, 2, 2, 32, 128), BF16),
            pltpu.VMEM((2, 2, 16, 32, 128), BF16),
            pltpu.VMEM((2, 2, 2, 8, 32, 128), BF16),
            pltpu.SemaphoreType.DMA((2, 12)),
            pltpu.SemaphoreType.DMA((2, 12)),
            pltpu.SemaphoreType.DMA((4,)),
        ],
        compiler_params=pltpu.CompilerParams(
            collective_id=0, has_side_effects=True, vmem_limit_bytes=40 * 2**20
        ),
        cost_estimate=pl.CostEstimate(flops=805306368, bytes_accessed=1638400, transcendentals=0),
    )(*(pltpu.with_memory_space_constraint(v, pltpu.HBM) for v in arrays))


def solution(mesh):
    return jax.shard_map(
        body,
        mesh=mesh,
        in_specs=(
            P("row", "col", None, None, None, None),
            P("row", "col", None),
            P(("col", "row"), None),
            P("col", None),
        ),
        out_specs=P("row", "col"),
        check_vma=False,
    )
```

```python
import jax
import jax.numpy as jnp
from jax import lax
from jax.experimental import pallas as pl
from jax.experimental.pallas import tpu as pltpu
from jax.sharding import PartitionSpec as P

MESH = pl.DeviceIdType.MESH
BF16 = jnp.bfloat16
F32 = jnp.float32
NY, NZH, NX = 8, 4, 4
Y_ORDER = (4, 3, 5, 2, 6, 1, 7)
Z_ORDER = (2, 1, 3)
PLANE_ORDER = (0, 1, 7, 2, 6, 3, 5, 4)
SCALE = 512.0**-0.5


def kernel(
    slot_hbm, mask_hbm, coeff_hbm, blocks_hbm, out_ref,
    slot_ref, mask_ref, coeff_ref, blocks,
    ga0, ga1, gb0, gb1, lhs, rhs, part, own, theirs, summed, landed, piece, mu, ya, zb, nua, nub, sends, recvs, from_z, from_y, from_plane, from_b, local,
):
    row, col = lax.axis_index("row"), lax.axis_index("col")
    ga, gb = (ga0, ga1), (gb0, gb1)
    y, zh = row // NZH, row % NZH
    chip, k = col // 2, col % 2
    zl, x = chip // NX, chip % NX

    def along_y(d):
        return (((y + d) % NY) * NZH + zh, col)

    def along_z(d):
        return (y * NZH + (zh + d) % NZH, col)

    def in_row(d):
        return (row, ((chip + d) % 8) * 2 + k)

    def along_x(d):
        return (row, (zl * NX + (x + d) % NX) * 2 + k)

    sibling = (row, chip * 2 + 1 - k)
    across = (1 - zl) * NX + x

    def send(src, dst, o, index, device, arrival=None):
        pltpu.make_async_remote_copy(
            src_ref=src, dst_ref=dst, send_sem=sends.at[o, index],
            recv_sem=recvs.at[o, index] if arrival is None else arrival,
            device_id=device, device_id_type=MESH,
        ).start()

    def took(sems, o, index, ref):
        pltpu.make_async_copy(ref, ref, sems.at[o, index]).wait()

    fetches = [
        pltpu.make_async_copy(src, dst, local.at[n])
        for n, (src, dst) in enumerate(
            ((coeff_hbm, coeff_ref), (slot_hbm, slot_ref), (mask_hbm, mask_ref), (blocks_hbm, blocks))
        )
    ]
    for fetch in fetches:
        fetch.start()
    barrier = pltpu.get_barrier_semaphore()
    peers = [along_y(d) for d in Y_ORDER] + [along_z(d) for d in Z_ORDER] + [in_row(d) for d in range(1, 8)] + [sibling]
    for peer in peers:
        pl.semaphore_signal(barrier, inc=1, device_id=peer, device_id_type=MESH)
    fetches[0].wait()
    for o in range(2):
        ga[o][y, zh] = coeff_ref[0:16, o * 128 : (o + 1) * 128]
        gb[o][zh, y] = coeff_ref[16:32, o * 128 : (o + 1) * 128]
    pl.semaphore_wait(barrier, len(peers))

    def pass_along_y(o, piece):
        for d in Y_ORDER:
            send(piece, piece, o, 2, along_y(d))

    def pass_along_z(o, piece):
        for d in Z_ORDER:
            send(piece, piece, o, 3, along_z(d))

    for o in range(2):
        mine = ga[o].at[y, zh]
        for d in Z_ORDER:
            send(mine, mine, o, 0, along_z(d), from_z.at[o, d - 1])
        mine = gb[o].at[zh, y]
        for d in Y_ORDER:
            send(mine, mine, o, 1, along_y(d), from_y.at[o, d - 1])
    for o in range(2):
        pass_along_y(o, ga[o].at[y, zh])
        pass_along_z(o, gb[o].at[zh, y])
    for fetch in fetches[1:]:
        fetch.wait()
    zero = jnp.zeros((256, 128), BF16)
    for mb in range(4):
        for s in range(8):
            here = (slot_ref[0, 0, s] >> 3) == mb
            lhs[mb, :, s * 128 : (s + 1) * 128] = jnp.where(here, blocks[s].reshape(256, 128), zero)
    for o in range(2):
        for d in (1, 7, 2, 6, 3, 5, 4):
            came = gb[o].at[zh, (y - d + NY) % NY]
            took(from_y, o, d - 1, came)
            pass_along_z(o, came)
    for o in range(2):
        for d in (1, 3, 2):
            came = ga[o].at[y, (zh - d + NZH) % NZH]
            took(from_z, o, d - 1, came)
            pass_along_y(o, came)

    def partial(o, first):
        left = lhs[pl.ds(first, 2)].reshape(512, 1024)
        return jnp.dot(left, rhs[o], preferred_element_type=F32).reshape(2, 2, 128, 128)

    def expand(o):
        took(recvs, o, 2, ga[o].at[pl.ds(0, 7)])
        took(recvs, o, 3, gb[o].at[pl.ds(0, 3)])
        for s in range(8):
            nb = slot_ref[0, 0, s] & 7
            rows = jnp.concatenate([ga[o][nb], gb[o][:, nb]], axis=1).reshape(128, 128)
            rhs[o, s * 128 : (s + 1) * 128, :] = jnp.where(mask_ref[o, nb] != 0, rows, jnp.zeros((128, 128), BF16))
        value = partial(o, (1 - k) * 2).astype(BF16)
        for j in range(2):
            for p in range(2):
                part[o, j * 128 : (j + 1) * 128, p * 128 : (p + 1) * 128] = value[j, p]
        send(part.at[o], theirs.at[o], o, 4, sibling)
        value = partial(o, k * 2)
        for j in range(2):
            for p in range(2):
                own[o, j * 128 : (j + 1) * 128, p * 128 : (p + 1) * 128] = value[j, p]
        landed[o, chip] = jnp.zeros((32, 256), BF16)
        took(recvs, o, 4, theirs.at[o])
        total = own[o] + theirs[o].astype(F32)
        own[o] = total
        summed[o] = total.astype(BF16).reshape(8, 32, 256)
        for d in (6, 2, 5, 7, 1, 3, 4):
            send(summed.at[o, (chip + d) % 8], landed.at[o, chip], o, 5, in_row(d))

    place = k * 8 + chip
    at_home, same_core = chip == y, k == zh // 2

    def deliver(src, dst, o, index, device, here):
        if here is None:
            send(src, dst, o, index, device)
            return

        @pl.when(here)
        def _():
            pltpu.make_async_copy(src, dst, recvs.at[o, index]).start()

        @pl.when(jnp.logical_not(here))
        def _():
            send(src, dst, o, index, device)

    for o in range(2):
        expand(o)
    for o in range(2):
        took(recvs, o, 5, landed.at[o, pl.ds(0, 7)])
        total = own[o, pl.ds(chip * 32, 32), :]
        for m in range(8):
            total = total + landed[o, m].astype(F32)
        total = total.astype(BF16)
        for p in range(2):
            block = total[:, p * 128 : (p + 1) * 128]
            piece[p, o] = block
            mu[p, o, place] = block
        ya[y, o] = total[:, 0:128]

    for dz in (2, 1, 3, 0):
        target = (chip * NZH + (zh + dz) % NZH, y * 2 + zh // 2)
        here = at_home & same_core if dz == 0 else None
        deliver(piece.at[1], zb.at[zh % 2, :, k], 0, 7, target, here)
    for d in Y_ORDER:
        send(ya.at[y], ya.at[y], 0, 6, along_y(d), from_plane.at[d - 1])
    send(piece, mu.at[:, :, place], 0, 12, (row, across * 2 + k))
    for d in (2, 1, 3):
        send(piece, mu.at[:, :, place], 0, 8, along_x(d))
    for d in PLANE_ORDER:
        yp = (y - d + NY) % NY
        if d:
            pltpu.make_async_copy(ya.at[yp], ya.at[yp], from_plane.at[d - 1]).wait()
        for dz in (2, 1, 3, 0):
            target = (y * NZH + (zh + dz) % NZH, yp * 2 + zh // 2)
            here = (chip == yp) & same_core if dz == 0 else None
            deliver(ya.at[yp], nua.at[zh % 2, :, place], 0, 10, target, here)
    took(recvs, 0, 12, mu.at[:, :, 0])
    came = mu.at[:, :, k * 8 + across]
    for d in (2, 1, 3):
        send(came, came, 0, 13, along_x(d))
    took(recvs, 0, 7, zb)
    for d in (3, 5, 2, 6, 1, 7):
        send(zb, nub.at[:, :, :, y], 0, 9, along_y(d), {3: from_b.at[0], 5: from_b.at[1]}.get(d))
    nub[:, :, :, y] = zb[...]
    for n, (d, on) in enumerate(((3, 1), (5, 7))):
        came = nub.at[:, :, :, (y - d + NY) % NY]
        pltpu.make_async_copy(came, came, from_b.at[n]).wait()
        came = nub.at[n, :, :, (y - d + NY) % NY]
        send(came, came, 0, 14, along_y(on))
    took(recvs, 0, 8, mu.at[:, :, pl.ds(0, 3)])
    took(recvs, 0, 13, mu.at[:, :, pl.ds(0, 3)])
    half = mu.at[:, :, pl.ds(k * 8, 8)]
    send(half, half, 0, 11, sibling)
    took(recvs, 0, 11, mu.at[:, :, pl.ds(0, 8)])
    took(recvs, 0, 9, nub.at[:, :, :, pl.ds(0, 4)])
    took(recvs, 0, 14, nub.at[:, :, :, 0])
    took(recvs, 0, 10, nua)

    def dot(left, right):
        return lax.dot_general(left, right, (((1,), (1,)), ((), ())), preferred_element_type=F32)

    left = jnp.concatenate([mu[p, o].reshape(512, 128) for p in range(2) for o in range(2)], axis=1)
    for h in range(2):
        for n in range(2):
            right = [nua[h, o, pl.ds(n * 8, 8)] for o in range(2)] + [nub[h, o, n] for o in range(2)]
            value = dot(left, jnp.concatenate([v.reshape(256, 128) for v in right], axis=1))
            out_ref[:, h * 512 + n * 256 : h * 512 + (n + 1) * 256] = (value * SCALE).astype(BF16)

    for o in range(2):
        took(sends, o, 0, ga[o].at[0, pl.ds(0, 3)])
        took(sends, o, 1, gb[o].at[0, pl.ds(0, 7)])
        took(sends, o, 2, ga[o].at[pl.ds(0, 7)])
        took(sends, o, 3, gb[o].at[pl.ds(0, 3)])
        took(sends, o, 4, theirs.at[o])
        took(sends, o, 5, landed.at[o, pl.ds(0, 7)])
    took(sends, 0, 6, ya.at[pl.ds(0, 7)])
    took(sends, 0, 8, mu.at[:, :, pl.ds(0, 3)])
    took(sends, 0, 12, mu.at[:, :, 0])
    took(sends, 0, 13, mu.at[:, :, pl.ds(0, 3)])
    took(sends, 0, 14, nub.at[:, :, :, 0])
    took(sends, 0, 9, nub.at[:, :, :, pl.ds(0, 6)])
    took(sends, 0, 11, mu.at[:, :, pl.ds(0, 8)])

    @pl.when(at_home & same_core)
    def _():
        took(sends, 0, 7, zb.at[:, :, 0])
        took(sends, 0, 7, zb.at[0, :, 0])

    @pl.when(jnp.logical_not(at_home & same_core))
    def _():
        took(sends, 0, 7, zb)

    @pl.when(same_core)
    def _():
        took(sends, 0, 10, nua.at[0, :, pl.ds(0, 15)])
        took(sends, 0, 10, nua.at[0])

    @pl.when(jnp.logical_not(same_core))
    def _():
        took(sends, 0, 10, nua)


def body(three_index, slot_pair, coeff, occ_mask):
    arrays = (slot_pair, occ_mask.T, coeff, three_index.reshape(8, 2, 128, 128))
    return pl.pallas_call(
        kernel,
        out_shape=jax.ShapeDtypeStruct((512, 1024), BF16),
        in_specs=[
            pl.BlockSpec(memory_space=pltpu.HBM),
            pl.BlockSpec(memory_space=pltpu.HBM),
            pl.BlockSpec(memory_space=pltpu.HBM),
            pl.BlockSpec(memory_space=pltpu.HBM),
        ],
        out_specs=pl.BlockSpec(memory_space=pltpu.VMEM),
        scratch_shapes=[
            pltpu.SMEM((1, 1, 8), jnp.int32),
            pltpu.SMEM((2, 8), jnp.int32),
            pltpu.VMEM((32, 256), BF16),
            pltpu.VMEM((8, 2, 128, 128), BF16),
            pltpu.VMEM((8, 4, 16, 128), BF16),
            pltpu.VMEM((8, 4, 16, 128), BF16),
            pltpu.VMEM((4, 8, 16, 128), BF16),
            pltpu.VMEM((4, 8, 16, 128), BF16),
            pltpu.VMEM((4, 256, 1024), BF16),
            pltpu.VMEM((2, 1024, 128), BF16),
            pltpu.VMEM((2, 256, 256), BF16),
            pltpu.VMEM((2, 256, 256), F32),
            pltpu.VMEM((2, 256, 256), BF16),
            pltpu.VMEM((2, 8, 32, 256), BF16),
            pltpu.VMEM((2, 8, 32, 256), BF16),
            pltpu.VMEM((2, 2, 32, 128), BF16),
            pltpu.VMEM((2, 2, 16, 32, 128), BF16),
            pltpu.VMEM((8, 2, 32, 128), BF16),
            pltpu.VMEM((2, 2, 2, 32, 128), BF16),
            pltpu.VMEM((2, 2, 16, 32, 128), BF16),
            pltpu.VMEM((2, 2, 2, 8, 32, 128), BF16),
            pltpu.SemaphoreType.DMA((2, 15)),
            pltpu.SemaphoreType.DMA((2, 15)),
            pltpu.SemaphoreType.DMA((2, 3)),
            pltpu.SemaphoreType.DMA((2, 7)),
            pltpu.SemaphoreType.DMA((7,)),
            pltpu.SemaphoreType.DMA((2,)),
            pltpu.SemaphoreType.DMA((4,)),
        ],
        compiler_params=pltpu.CompilerParams(
            collective_id=0, has_side_effects=True, vmem_limit_bytes=40 * 2**20
        ),
        cost_estimate=pl.CostEstimate(flops=805306368, bytes_accessed=1638400, transcendentals=0),
    )(*(pltpu.with_memory_space_constraint(v, pltpu.HBM) for v in arrays))


def solution(mesh):
    return jax.shard_map(
        body,
        mesh=mesh,
        in_specs=(
            P("row", "col", None, None, None, None),
            P("row", "col", None),
            P(("col", "row"), None),
            P("col", None),
        ),
        out_specs=P("row", "col"),
        check_vma=False,
    )
```

```python
import jax
import jax.numpy as jnp
from jax import lax
from jax.experimental import pallas as pl
from jax.experimental.pallas import tpu as pltpu
from jax.sharding import PartitionSpec as P

MESH = pl.DeviceIdType.MESH
BF16 = jnp.bfloat16
F32 = jnp.float32
NY, NZH, NX = 8, 4, 4
Y_ORDER = (4, 3, 5, 2, 6, 1, 7)
Z_ORDER = (2, 1, 3)
PLANE_ORDER = (0, 1, 7, 2, 6, 3, 5, 4)
SCALE = 512.0**-0.5


def kernel(
    slot_hbm, mask_hbm, coeff_hbm, blocks_hbm, out_ref,
    slot_ref, mask_ref, coeff_ref, blocks,
    ga0, ga1, gb0, gb1, lhs, rhs, part, own, theirs, summed, landed, piece, mu, ya, zb, nua, nub, sends, recvs, from_z, from_y, from_plane, from_b, local,
):
    row, col = lax.axis_index("row"), lax.axis_index("col")
    ga, gb = (ga0, ga1), (gb0, gb1)
    y, zh = row // NZH, row % NZH
    chip, k = col // 2, col % 2
    zl, x = chip // NX, chip % NX

    def along_y(d):
        return (((y + d) % NY) * NZH + zh, col)

    def along_z(d):
        return (y * NZH + (zh + d) % NZH, col)

    def in_row(d):
        return (row, ((chip + d) % 8) * 2 + k)

    def along_x(d):
        return (row, (zl * NX + (x + d) % NX) * 2 + k)

    sibling = (row, chip * 2 + 1 - k)
    across = (1 - zl) * NX + x

    def send(src, dst, o, index, device, arrival=None):
        pltpu.make_async_remote_copy(
            src_ref=src, dst_ref=dst, send_sem=sends.at[o, index],
            recv_sem=recvs.at[o, index] if arrival is None else arrival,
            device_id=device, device_id_type=MESH,
        ).start()

    def took(sems, o, index, ref):
        pltpu.make_async_copy(ref, ref, sems.at[o, index]).wait()

    fetches = [
        pltpu.make_async_copy(src, dst, local.at[n])
        for n, (src, dst) in enumerate(
            ((coeff_hbm, coeff_ref), (slot_hbm, slot_ref), (mask_hbm, mask_ref), (blocks_hbm, blocks))
        )
    ]
    for fetch in fetches:
        fetch.start()
    barrier = pltpu.get_barrier_semaphore()
    peers = [along_y(d) for d in Y_ORDER] + [along_z(d) for d in Z_ORDER] + [in_row(d) for d in range(1, 8)] + [sibling]
    for peer in peers:
        pl.semaphore_signal(barrier, inc=1, device_id=peer, device_id_type=MESH)
    fetches[0].wait()
    for o in range(2):
        ga[o][y, zh] = coeff_ref[0:16, o * 128 : (o + 1) * 128]
        gb[o][zh, y] = coeff_ref[16:32, o * 128 : (o + 1) * 128]
    pl.semaphore_wait(barrier, len(peers))

    def pass_along_y(o, piece):
        for d in Y_ORDER:
            send(piece, piece, o, 2, along_y(d))

    def pass_along_z(o, piece):
        for d in Z_ORDER:
            send(piece, piece, o, 3, along_z(d))

    for o in range(2):
        mine = ga[o].at[y, zh]
        for d in Z_ORDER:
            send(mine, mine, o, 0, along_z(d), from_z.at[o, d - 1])
        mine = gb[o].at[zh, y]
        for d in Y_ORDER:
            send(mine, mine, o, 1, along_y(d), from_y.at[o, d - 1])
    for o in range(2):
        pass_along_y(o, ga[o].at[y, zh])
        pass_along_z(o, gb[o].at[zh, y])
    for fetch in fetches[1:]:
        fetch.wait()
    zero = jnp.zeros((256, 128), BF16)
    for mb in range(4):
        for s in range(8):
            here = (slot_ref[0, 0, s] >> 3) == mb
            lhs[mb, :, s * 128 : (s + 1) * 128] = jnp.where(here, blocks[s].reshape(256, 128), zero)
    for o in range(2):
        for d in (1, 7, 2, 6, 3, 5, 4):
            came = gb[o].at[zh, (y - d + NY) % NY]
            took(from_y, o, d - 1, came)
            pass_along_z(o, came)
    for o in range(2):
        for d in (1, 3, 2):
            came = ga[o].at[y, (zh - d + NZH) % NZH]
            took(from_z, o, d - 1, came)
            pass_along_y(o, came)

    def partial(o, first):
        left = lhs[pl.ds(first, 2)].reshape(512, 1024)
        return jnp.dot(left, rhs[o], preferred_element_type=F32).reshape(2, 2, 128, 128)

    def expand(o):
        took(recvs, o, 2, ga[o].at[pl.ds(0, 7)])
        took(recvs, o, 3, gb[o].at[pl.ds(0, 3)])
        for s in range(8):
            nb = slot_ref[0, 0, s] & 7
            rows = jnp.concatenate([ga[o][nb], gb[o][:, nb]], axis=1).reshape(128, 128)
            rhs[o, s * 128 : (s + 1) * 128, :] = jnp.where(mask_ref[o, nb] != 0, rows, jnp.zeros((128, 128), BF16))
        value = partial(o, (1 - k) * 2).astype(BF16)
        for j in range(2):
            for p in range(2):
                part[o, j * 128 : (j + 1) * 128, p * 128 : (p + 1) * 128] = value[j, p]
        send(part.at[o], theirs.at[o], o, 4, sibling)
        value = partial(o, k * 2)
        for j in range(2):
            for p in range(2):
                own[o, j * 128 : (j + 1) * 128, p * 128 : (p + 1) * 128] = value[j, p]
        landed[o, chip] = jnp.zeros((32, 256), BF16)
        took(recvs, o, 4, theirs.at[o])
        total = own[o] + theirs[o].astype(F32)
        own[o] = total
        summed[o] = total.astype(BF16).reshape(8, 32, 256)
        for d in (6, 2, 5, 7, 1, 3, 4):
            send(summed.at[o, (chip + d) % 8], landed.at[o, chip], o, 5, in_row(d))

    place = k * 8 + chip
    at_home, same_core = chip == y, k == zh // 2

    def deliver(src, dst, o, index, device, here):
        if here is None:
            send(src, dst, o, index, device)
            return

        @pl.when(here)
        def _():
            pltpu.make_async_copy(src, dst, recvs.at[o, index]).start()

        @pl.when(jnp.logical_not(here))
        def _():
            send(src, dst, o, index, device)

    for o in range(2):
        expand(o)
    for o in range(2):
        took(recvs, o, 5, landed.at[o, pl.ds(0, 7)])
        total = own[o, pl.ds(chip * 32, 32), :]
        for m in range(8):
            total = total + landed[o, m].astype(F32)
        total = total.astype(BF16)
        for p in range(2):
            block = total[:, p * 128 : (p + 1) * 128]
            piece[p, o] = block
            mu[p, o, place] = block
        ya[y, o] = total[:, 0:128]

    for dz in (2, 1, 3, 0):
        target = (chip * NZH + (zh + dz) % NZH, y * 2 + zh // 2)
        here = at_home & same_core if dz == 0 else None
        deliver(piece.at[1], zb.at[zh % 2, :, k], 0, 7, target, here)
    for d in Y_ORDER:
        send(ya.at[y], ya.at[y], 0, 6, along_y(d), from_plane.at[d - 1])
    send(piece, mu.at[:, :, place], 0, 12, (row, across * 2 + k))
    for d in (2, 1, 3):
        send(piece, mu.at[:, :, place], 0, 8, along_x(d))
    for d in PLANE_ORDER:
        yp = (y - d + NY) % NY
        if d:
            pltpu.make_async_copy(ya.at[yp], ya.at[yp], from_plane.at[d - 1]).wait()
        for dz in (1, 3, 0, 2):
            target = (y * NZH + (zh + dz) % NZH, yp * 2 + zh // 2)
            here = (chip == yp) & same_core if dz == 0 else None
            deliver(ya.at[yp], nua.at[zh % 2, :, place], 0, 10, target, here)
    took(recvs, 0, 12, mu.at[:, :, 0])
    came = mu.at[:, :, k * 8 + across]
    for d in (2, 1, 3):
        send(came, came, 0, 13, along_x(d))
    took(recvs, 0, 7, zb)
    for d in (3, 5, 1, 7, 2, 6):
        send(zb, nub.at[:, :, :, y], 0, 9, along_y(d), {3: from_b.at[0], 5: from_b.at[1]}.get(d))
    nub[:, :, :, y] = zb[...]
    for n, (d, on) in enumerate(((3, 1), (5, 7))):
        came = nub.at[:, :, :, (y - d + NY) % NY]
        pltpu.make_async_copy(came, came, from_b.at[n]).wait()
        came = nub.at[n, :, :, (y - d + NY) % NY]
        send(came, came, 0, 14, along_y(on))
    took(recvs, 0, 8, mu.at[:, :, pl.ds(0, 3)])
    took(recvs, 0, 13, mu.at[:, :, pl.ds(0, 3)])
    half = mu.at[:, :, pl.ds(k * 8, 8)]
    send(half, half, 0, 11, sibling)
    took(recvs, 0, 11, mu.at[:, :, pl.ds(0, 8)])
    took(recvs, 0, 9, nub.at[:, :, :, pl.ds(0, 4)])
    took(recvs, 0, 14, nub.at[:, :, :, 0])
    took(recvs, 0, 10, nua)

    def dot(left, right):
        return lax.dot_general(left, right, (((1,), (1,)), ((), ())), preferred_element_type=F32)

    left = jnp.concatenate([mu[p, o].reshape(512, 128) for p in range(2) for o in range(2)], axis=1)
    for h in range(2):
        for n in range(2):
            right = [nua[h, o, pl.ds(n * 8, 8)] for o in range(2)] + [nub[h, o, n] for o in range(2)]
            value = dot(left, jnp.concatenate([v.reshape(256, 128) for v in right], axis=1))
            out_ref[:, h * 512 + n * 256 : h * 512 + (n + 1) * 256] = (value * SCALE).astype(BF16)

    for o in range(2):
        took(sends, o, 0, ga[o].at[0, pl.ds(0, 3)])
        took(sends, o, 1, gb[o].at[0, pl.ds(0, 7)])
        took(sends, o, 2, ga[o].at[pl.ds(0, 7)])
        took(sends, o, 3, gb[o].at[pl.ds(0, 3)])
        took(sends, o, 4, theirs.at[o])
        took(sends, o, 5, landed.at[o, pl.ds(0, 7)])
    took(sends, 0, 6, ya.at[pl.ds(0, 7)])
    took(sends, 0, 8, mu.at[:, :, pl.ds(0, 3)])
    took(sends, 0, 12, mu.at[:, :, 0])
    took(sends, 0, 13, mu.at[:, :, pl.ds(0, 3)])
    took(sends, 0, 14, nub.at[:, :, :, 0])
    took(sends, 0, 9, nub.at[:, :, :, pl.ds(0, 6)])
    took(sends, 0, 11, mu.at[:, :, pl.ds(0, 8)])

    @pl.when(at_home & same_core)
    def _():
        took(sends, 0, 7, zb.at[:, :, 0])
        took(sends, 0, 7, zb.at[0, :, 0])

    @pl.when(jnp.logical_not(at_home & same_core))
    def _():
        took(sends, 0, 7, zb)

    @pl.when(same_core)
    def _():
        took(sends, 0, 10, nua.at[0, :, pl.ds(0, 15)])
        took(sends, 0, 10, nua.at[0])

    @pl.when(jnp.logical_not(same_core))
    def _():
        took(sends, 0, 10, nua)


def body(three_index, slot_pair, coeff, occ_mask):
    arrays = (slot_pair, occ_mask.T, coeff, three_index.reshape(8, 2, 128, 128))
    return pl.pallas_call(
        kernel,
        out_shape=jax.ShapeDtypeStruct((512, 1024), BF16),
        in_specs=[
            pl.BlockSpec(memory_space=pltpu.HBM),
            pl.BlockSpec(memory_space=pltpu.HBM),
            pl.BlockSpec(memory_space=pltpu.HBM),
            pl.BlockSpec(memory_space=pltpu.HBM),
        ],
        out_specs=pl.BlockSpec(memory_space=pltpu.VMEM),
        scratch_shapes=[
            pltpu.SMEM((1, 1, 8), jnp.int32),
            pltpu.SMEM((2, 8), jnp.int32),
            pltpu.VMEM((32, 256), BF16),
            pltpu.VMEM((8, 2, 128, 128), BF16),
            pltpu.VMEM((8, 4, 16, 128), BF16),
            pltpu.VMEM((8, 4, 16, 128), BF16),
            pltpu.VMEM((4, 8, 16, 128), BF16),
            pltpu.VMEM((4, 8, 16, 128), BF16),
            pltpu.VMEM((4, 256, 1024), BF16),
            pltpu.VMEM((2, 1024, 128), BF16),
            pltpu.VMEM((2, 256, 256), BF16),
            pltpu.VMEM((2, 256, 256), F32),
            pltpu.VMEM((2, 256, 256), BF16),
            pltpu.VMEM((2, 8, 32, 256), BF16),
            pltpu.VMEM((2, 8, 32, 256), BF16),
            pltpu.VMEM((2, 2, 32, 128), BF16),
            pltpu.VMEM((2, 2, 16, 32, 128), BF16),
            pltpu.VMEM((8, 2, 32, 128), BF16),
            pltpu.VMEM((2, 2, 2, 32, 128), BF16),
            pltpu.VMEM((2, 2, 16, 32, 128), BF16),
            pltpu.VMEM((2, 2, 2, 8, 32, 128), BF16),
            pltpu.SemaphoreType.DMA((2, 15)),
            pltpu.SemaphoreType.DMA((2, 15)),
            pltpu.SemaphoreType.DMA((2, 3)),
            pltpu.SemaphoreType.DMA((2, 7)),
            pltpu.SemaphoreType.DMA((7,)),
            pltpu.SemaphoreType.DMA((2,)),
            pltpu.SemaphoreType.DMA((4,)),
        ],
        compiler_params=pltpu.CompilerParams(
            collective_id=0, has_side_effects=True, vmem_limit_bytes=40 * 2**20
        ),
        cost_estimate=pl.CostEstimate(flops=805306368, bytes_accessed=1638400, transcendentals=0),
    )(*(pltpu.with_memory_space_constraint(v, pltpu.HBM) for v in arrays))


def solution(mesh):
    return jax.shard_map(
        body,
        mesh=mesh,
        in_specs=(
            P("row", "col", None, None, None, None),
            P("row", "col", None),
            P(("col", "row"), None),
            P("col", None),
        ),
        out_specs=P("row", "col"),
        check_vma=False,
    )
```

```python
import jax
import jax.numpy as jnp
from jax import lax
from jax.experimental import pallas as pl
from jax.experimental.pallas import tpu as pltpu
from jax.sharding import PartitionSpec as P

MESH = pl.DeviceIdType.MESH
BF16 = jnp.bfloat16
F32 = jnp.float32
NY, NZH, NX = 8, 4, 4
Y_ORDER = (4, 3, 5, 2, 6, 1, 7)
Z_ORDER = (2, 1, 3)
PLANE_ORDER = (0, 1, 7, 2, 6, 3, 5, 4)
SCALE = 512.0**-0.5


def kernel(
    slot_hbm, mask_hbm, coeff_hbm, blocks_hbm, out_ref,
    slot_ref, mask_ref, coeff_ref, blocks,
    ga0, ga1, gb0, gb1, lhs, rhs, part, own, theirs, summed, landed, piece, mu, ya, zb, nua, nub, early, sends, recvs, from_z, from_y, from_plane, from_b, local,
):
    row, col = lax.axis_index("row"), lax.axis_index("col")
    ga, gb = (ga0, ga1), (gb0, gb1)
    y, zh = row // NZH, row % NZH
    chip, k = col // 2, col % 2
    zl, x = chip // NX, chip % NX

    def along_y(d):
        return (((y + d) % NY) * NZH + zh, col)

    def along_z(d):
        return (y * NZH + (zh + d) % NZH, col)

    def in_row(d):
        return (row, ((chip + d) % 8) * 2 + k)

    def along_x(d):
        return (row, (zl * NX + (x + d) % NX) * 2 + k)

    sibling = (row, chip * 2 + 1 - k)
    across = (1 - zl) * NX + x

    def send(src, dst, o, index, device, arrival=None):
        pltpu.make_async_remote_copy(
            src_ref=src, dst_ref=dst, send_sem=sends.at[o, index],
            recv_sem=recvs.at[o, index] if arrival is None else arrival,
            device_id=device, device_id_type=MESH,
        ).start()

    def took(sems, o, index, ref):
        pltpu.make_async_copy(ref, ref, sems.at[o, index]).wait()

    fetches = [
        pltpu.make_async_copy(src, dst, local.at[n])
        for n, (src, dst) in enumerate(
            ((coeff_hbm, coeff_ref), (slot_hbm, slot_ref), (mask_hbm, mask_ref), (blocks_hbm, blocks))
        )
    ]
    for fetch in fetches:
        fetch.start()
    barrier = pltpu.get_barrier_semaphore()
    peers = [along_y(d) for d in Y_ORDER] + [along_z(d) for d in Z_ORDER] + [in_row(d) for d in range(1, 8)] + [sibling]
    for peer in peers:
        pl.semaphore_signal(barrier, inc=1, device_id=peer, device_id_type=MESH)
    fetches[0].wait()
    for o in range(2):
        ga[o][y, zh] = coeff_ref[0:16, o * 128 : (o + 1) * 128]
        gb[o][zh, y] = coeff_ref[16:32, o * 128 : (o + 1) * 128]
    pl.semaphore_wait(barrier, len(peers))

    def pass_along_y(o, piece):
        for d in Y_ORDER:
            send(piece, piece, o, 2, along_y(d))

    def pass_along_z(o, piece):
        for d in Z_ORDER:
            send(piece, piece, o, 3, along_z(d))

    for o in range(2):
        mine = ga[o].at[y, zh]
        for d in Z_ORDER:
            send(mine, mine, o, 0, along_z(d), from_z.at[o, d - 1])
        mine = gb[o].at[zh, y]
        for d in Y_ORDER:
            send(mine, mine, o, 1, along_y(d), from_y.at[o, d - 1])
    for o in range(2):
        pass_along_y(o, ga[o].at[y, zh])
        pass_along_z(o, gb[o].at[zh, y])
    for fetch in fetches[1:]:
        fetch.wait()
    zero = jnp.zeros((256, 128), BF16)
    for mb in range(4):
        for s in range(8):
            here = (slot_ref[0, 0, s] >> 3) == mb
            lhs[mb, :, s * 128 : (s + 1) * 128] = jnp.where(here, blocks[s].reshape(256, 128), zero)
    for o in range(2):
        for d in (1, 7, 2, 6, 3, 5, 4):
            came = gb[o].at[zh, (y - d + NY) % NY]
            took(from_y, o, d - 1, came)
            pass_along_z(o, came)
    for o in range(2):
        for d in (1, 3, 2):
            came = ga[o].at[y, (zh - d + NZH) % NZH]
            took(from_z, o, d - 1, came)
            pass_along_y(o, came)

    def partial(o, first):
        left = lhs[pl.ds(first, 2)].reshape(512, 1024)
        return jnp.dot(left, rhs[o], preferred_element_type=F32).reshape(2, 2, 128, 128)

    def expand(o):
        took(recvs, o, 2, ga[o].at[pl.ds(0, 7)])
        took(recvs, o, 3, gb[o].at[pl.ds(0, 3)])
        for s in range(8):
            nb = slot_ref[0, 0, s] & 7
            rows = jnp.concatenate([ga[o][nb], gb[o][:, nb]], axis=1).reshape(128, 128)
            rhs[o, s * 128 : (s + 1) * 128, :] = jnp.where(mask_ref[o, nb] != 0, rows, jnp.zeros((128, 128), BF16))
        value = partial(o, (1 - k) * 2).astype(BF16)
        for j in range(2):
            for p in range(2):
                part[o, j * 128 : (j + 1) * 128, p * 128 : (p + 1) * 128] = value[j, p]
        send(part.at[o], theirs.at[o], o, 4, sibling)
        value = partial(o, k * 2)
        for j in range(2):
            for p in range(2):
                own[o, j * 128 : (j + 1) * 128, p * 128 : (p + 1) * 128] = value[j, p]
        landed[o, chip] = jnp.zeros((32, 256), BF16)
        took(recvs, o, 4, theirs.at[o])
        total = own[o] + theirs[o].astype(F32)
        own[o] = total
        summed[o] = total.astype(BF16).reshape(8, 32, 256)
        for d in (6, 2, 5, 7, 1, 3, 4):
            send(summed.at[o, (chip + d) % 8], landed.at[o, chip], o, 5, in_row(d))

    place = k * 8 + chip
    at_home, same_core = chip == y, k == zh // 2

    def deliver(src, dst, o, index, device, here):
        if here is None:
            send(src, dst, o, index, device)
            return

        @pl.when(here)
        def _():
            pltpu.make_async_copy(src, dst, recvs.at[o, index]).start()

        @pl.when(jnp.logical_not(here))
        def _():
            send(src, dst, o, index, device)

    for o in range(2):
        expand(o)
    for o in range(2):
        took(recvs, o, 5, landed.at[o, pl.ds(0, 7)])
        total = own[o, pl.ds(chip * 32, 32), :]
        for m in range(8):
            total = total + landed[o, m].astype(F32)
        total = total.astype(BF16)
        for p in range(2):
            block = total[:, p * 128 : (p + 1) * 128]
            piece[p, o] = block
            mu[p, o, place] = block
        ya[y, o] = total[:, 0:128]

    for dz in (2, 1, 3, 0):
        target = (chip * NZH + (zh + dz) % NZH, y * 2 + zh // 2)
        here = at_home & same_core if dz == 0 else None
        deliver(piece.at[1], zb.at[zh % 2, :, k], 0, 7, target, here)
    for d in Y_ORDER:
        send(ya.at[y], ya.at[y], 0, 6, along_y(d), from_plane.at[d - 1])
    send(piece, mu.at[:, :, place], 0, 12, (row, across * 2 + k))
    for d in (2, 1, 3):
        send(piece, mu.at[:, :, place], 0, 8, along_x(d))
    for d in PLANE_ORDER:
        yp = (y - d + NY) % NY
        if d:
            pltpu.make_async_copy(ya.at[yp], ya.at[yp], from_plane.at[d - 1]).wait()
        for dz in (1, 3, 0, 2):
            target = (y * NZH + (zh + dz) % NZH, yp * 2 + zh // 2)
            here = (chip == yp) & same_core if dz == 0 else None
            deliver(ya.at[yp], nua.at[zh % 2, :, place], 0, 10, target, here)
    took(recvs, 0, 12, mu.at[:, :, 0])
    came = mu.at[:, :, k * 8 + across]
    for d in (2, 1, 3):
        send(came, came, 0, 13, along_x(d))
    took(recvs, 0, 7, zb)
    for d in (3, 5, 1, 7, 2, 6):
        send(zb, nub.at[:, :, :, y], 0, 9, along_y(d), {3: from_b.at[0], 5: from_b.at[1]}.get(d))
    nub[:, :, :, y] = zb[...]
    for n, (d, on) in enumerate(((3, 1), (5, 7))):
        came = nub.at[:, :, :, (y - d + NY) % NY]
        pltpu.make_async_copy(came, came, from_b.at[n]).wait()
        came = nub.at[n, :, :, (y - d + NY) % NY]
        send(came, came, 0, 14, along_y(on))
    took(recvs, 0, 8, mu.at[:, :, pl.ds(0, 3)])
    took(recvs, 0, 13, mu.at[:, :, pl.ds(0, 3)])
    half = mu.at[:, :, pl.ds(k * 8, 8)]
    send(half, half, 0, 11, sibling)
    took(recvs, 0, 11, mu.at[:, :, pl.ds(0, 8)])
    took(recvs, 0, 9, nub.at[:, :, :, pl.ds(0, 4)])
    took(recvs, 0, 14, nub.at[:, :, :, 0])

    def dot(left, right):
        return lax.dot_general(left, right, (((1,), (1,)), ((), ())), preferred_element_type=F32)

    def left(p):
        return jnp.concatenate([mu[p, o].reshape(512, 128) for o in range(2)], axis=1)

    for h in range(2):
        for n in range(2):
            right = jnp.concatenate([nub[h, o, n].reshape(256, 128) for o in range(2)], axis=1)
            early[h, n] = dot(left(1), right)
    took(recvs, 0, 10, nua)
    for h in range(2):
        for n in range(2):
            right = [nua[h, o, pl.ds(n * 8, 8)].reshape(256, 128) for o in range(2)]
            value = early[h, n] + dot(left(0), jnp.concatenate(right, axis=1))
            out_ref[:, h * 512 + n * 256 : h * 512 + (n + 1) * 256] = (value * SCALE).astype(BF16)

    for o in range(2):
        took(sends, o, 0, ga[o].at[0, pl.ds(0, 3)])
        took(sends, o, 1, gb[o].at[0, pl.ds(0, 7)])
        took(sends, o, 2, ga[o].at[pl.ds(0, 7)])
        took(sends, o, 3, gb[o].at[pl.ds(0, 3)])
        took(sends, o, 4, theirs.at[o])
        took(sends, o, 5, landed.at[o, pl.ds(0, 7)])
    took(sends, 0, 6, ya.at[pl.ds(0, 7)])
    took(sends, 0, 8, mu.at[:, :, pl.ds(0, 3)])
    took(sends, 0, 12, mu.at[:, :, 0])
    took(sends, 0, 13, mu.at[:, :, pl.ds(0, 3)])
    took(sends, 0, 14, nub.at[:, :, :, 0])
    took(sends, 0, 9, nub.at[:, :, :, pl.ds(0, 6)])
    took(sends, 0, 11, mu.at[:, :, pl.ds(0, 8)])

    @pl.when(at_home & same_core)
    def _():
        took(sends, 0, 7, zb.at[:, :, 0])
        took(sends, 0, 7, zb.at[0, :, 0])

    @pl.when(jnp.logical_not(at_home & same_core))
    def _():
        took(sends, 0, 7, zb)

    @pl.when(same_core)
    def _():
        took(sends, 0, 10, nua.at[0, :, pl.ds(0, 15)])
        took(sends, 0, 10, nua.at[0])

    @pl.when(jnp.logical_not(same_core))
    def _():
        took(sends, 0, 10, nua)


def body(three_index, slot_pair, coeff, occ_mask):
    arrays = (slot_pair, occ_mask.T, coeff, three_index.reshape(8, 2, 128, 128))
    return pl.pallas_call(
        kernel,
        out_shape=jax.ShapeDtypeStruct((512, 1024), BF16),
        in_specs=[
            pl.BlockSpec(memory_space=pltpu.HBM),
            pl.BlockSpec(memory_space=pltpu.HBM),
            pl.BlockSpec(memory_space=pltpu.HBM),
            pl.BlockSpec(memory_space=pltpu.HBM),
        ],
        out_specs=pl.BlockSpec(memory_space=pltpu.VMEM),
        scratch_shapes=[
            pltpu.SMEM((1, 1, 8), jnp.int32),
            pltpu.SMEM((2, 8), jnp.int32),
            pltpu.VMEM((32, 256), BF16),
            pltpu.VMEM((8, 2, 128, 128), BF16),
            pltpu.VMEM((8, 4, 16, 128), BF16),
            pltpu.VMEM((8, 4, 16, 128), BF16),
            pltpu.VMEM((4, 8, 16, 128), BF16),
            pltpu.VMEM((4, 8, 16, 128), BF16),
            pltpu.VMEM((4, 256, 1024), BF16),
            pltpu.VMEM((2, 1024, 128), BF16),
            pltpu.VMEM((2, 256, 256), BF16),
            pltpu.VMEM((2, 256, 256), F32),
            pltpu.VMEM((2, 256, 256), BF16),
            pltpu.VMEM((2, 8, 32, 256), BF16),
            pltpu.VMEM((2, 8, 32, 256), BF16),
            pltpu.VMEM((2, 2, 32, 128), BF16),
            pltpu.VMEM((2, 2, 16, 32, 128), BF16),
            pltpu.VMEM((8, 2, 32, 128), BF16),
            pltpu.VMEM((2, 2, 2, 32, 128), BF16),
            pltpu.VMEM((2, 2, 16, 32, 128), BF16),
            pltpu.VMEM((2, 2, 2, 8, 32, 128), BF16),
            pltpu.VMEM((2, 2, 512, 256), F32),
            pltpu.SemaphoreType.DMA((2, 15)),
            pltpu.SemaphoreType.DMA((2, 15)),
            pltpu.SemaphoreType.DMA((2, 3)),
            pltpu.SemaphoreType.DMA((2, 7)),
            pltpu.SemaphoreType.DMA((7,)),
            pltpu.SemaphoreType.DMA((2,)),
            pltpu.SemaphoreType.DMA((4,)),
        ],
        compiler_params=pltpu.CompilerParams(
            collective_id=0, has_side_effects=True, vmem_limit_bytes=40 * 2**20
        ),
        cost_estimate=pl.CostEstimate(flops=805306368, bytes_accessed=1638400, transcendentals=0),
    )(*(pltpu.with_memory_space_constraint(v, pltpu.HBM) for v in arrays))


def solution(mesh):
    return jax.shard_map(
        body,
        mesh=mesh,
        in_specs=(
            P("row", "col", None, None, None, None),
            P("row", "col", None),
            P(("col", "row"), None),
            P("col", None),
        ),
        out_specs=P("row", "col"),
        check_vma=False,
    )
```
